32 devices in a mesh: sec: 4 (over y, core), op: 8 (over z, x).
Axes of the slice: x: 2, y: 2, z: 4, core: 2. Of those that a mesh axis runs over, the one named last changes fastest.
Arguments:
- wavefunction: bfloat16 [4, 2, 384, 384], P('sec', None, 'op'), may hold values from -6 to 6
- diagonal: float32 [4, 384, 384], P('sec', 'op'), may hold values from 0.5 to 2
- left_ops: bfloat16 [128, 384, 384], P(('sec', 'op')), may hold values from -0.0390625 to 0.0390625
- right_ops: bfloat16 [128, 384, 384], P(('sec', 'op')), may hold values from -0.3125 to 0.3125
- offsets: int32 [128, 2], P(('sec', 'op')), may hold values from 0 to 1
Outputs:
- preconditioned: bfloat16 [4, 2, 384, 384], P('sec', None, 'op')
The draws below stay inside these ranges and needn't reach their ends.
All inputs are finite; a program needn't handle non-finite values.
Results may differ from the reference program's by a relative error of at most 0.025.
Values may be sent and summed in bfloat16 or wider, within the bound.
No kernel may reach another device: no remote copies, remote signals or barrier semaphores. Data moves between devices by JAX's collectives and lax.ppermute only.
A program may use at most 64 MiB of HBM per device.

```python
import math
import jax
import jax.numpy as jnp
from jax import lax

B = 384
ROOTS = 2
PAIRS = 4
ITERS = 2
SECTORS = 4
GROUP_PAIRS = 32
PAIRS_ALL = 128
N_OP = 8


def with_ends(entries, key, low, largest):
    spot = [jax.random.randint(jax.random.fold_in(key, axis), (), 0, length) for axis, length in enumerate(entries.shape)]
    widest = entries.shape.index(max(entries.shape))
    beside = spot[:widest] + [(spot[widest] + 1) % entries.shape[widest]] + spot[widest + 1:]
    return entries.at[tuple(spot)].set(low).at[tuple(beside)].set(largest)


def block_levels(rng, shape, pieces, smallest, largest):
    def one(position, blocks):
        steps = jax.random.uniform(jax.random.fold_in(jax.random.fold_in(rng, 6), position), (blocks,), jnp.float32, smallest / len(pieces), largest / len(pieces))
        return jnp.repeat(jnp.exp(steps), shape[position] // blocks).reshape((-1,) + (1,) * (len(shape) - position - 1))

    factor_of = one(*pieces[0])
    for cut in pieces[1:]:
        factor_of = factor_of * one(*cut)
    return factor_of


def normal_values(rng, shape, scale, most, pieces=(), kind=jnp.bfloat16):
    factor_of = block_levels(rng, shape, pieces, -0.22, 0.18) if pieces else 1.0
    entries = jax.random.normal(rng, shape, jnp.float32) * scale * factor_of
    return jnp.minimum(jnp.maximum(entries, -most), most).astype(kind)


def setup_inputs(seed: int = 0) -> dict:
    key_list = jax.random.split(jax.random.key(seed), 6)
    wavefunction = normal_values(key_list[0], (SECTORS, ROOTS, B, B), 1.0, 6.0, ((0, 4), (2, 8)))
    diagonal = jnp.clip(jnp.exp(math.log(2.0) - 1.3862944 * jax.random.uniform(key_list[1], (SECTORS, B, B), jnp.float32) ** block_levels(key_list[1], (SECTORS, B, B), ((0, 4), (1, 8)), -0.2, 0.2)), 0.5, 2.0)
    left_ops = normal_values(key_list[2], (PAIRS_ALL, B, B), (2 * B * GROUP_PAIRS) ** -0.5, 0.0390625, ((0, 32),))
    right_ops = normal_values(key_list[3], (PAIRS_ALL, B, B), B ** -0.5, 0.3125, ((0, 32),))
    offsets = with_ends(jax.random.randint(key_list[4], (PAIRS_ALL, 2), 0, 2), jax.random.fold_in(key_list[4], 1), 0, 1).astype(jnp.int32)
    return {"wavefunction": wavefunction, "diagonal": diagonal, "left_ops": left_ops, "right_ops": right_ops, "offsets": offsets}


def partials(vector, left_ops, right_ops, offsets):
    vector_f = vector.astype(jnp.float32)
    right_f = right_ops.astype(jnp.float32)
    left_f = left_ops.astype(jnp.float32)
    turned = jnp.einsum('xab,pcb->pxac', vector_f, right_f).astype(jnp.bfloat16).astype(jnp.float32)
    plain_rows = jnp.einsum('xab,pbc->pxac', vector_f, right_f).astype(jnp.bfloat16).astype(jnp.float32)
    raise_mask = (offsets[:, 0] == 1).astype(jnp.float32)[:, None, None]
    lower_mask = (offsets[:, 1] == 1).astype(jnp.float32)[:, None, None]
    raised = jnp.einsum('pab,pxbc->xac', left_f * raise_mask, turned)
    staying = jnp.einsum('pab,pxbc->xac', left_f * (1.0 - raise_mask), turned)
    staying = staying + jnp.einsum('pba,pxbc->xac', left_f * (1.0 - lower_mask), plain_rows)
    lowered = jnp.einsum('pba,pxbc->xac', left_f * lower_mask, plain_rows)
    return jnp.stack([lowered.astype(jnp.bfloat16), staying.astype(jnp.bfloat16), raised.astype(jnp.bfloat16)])


def apply_sigma(vectors, left_ops, right_ops, offsets):
    groups = PAIRS_ALL // PAIRS

    def add_group(accumulated, group):
        sector = (group // N_OP).astype(jnp.int32)
        first = (group * PAIRS).astype(jnp.int32)
        left_group = lax.dynamic_slice_in_dim(left_ops, first, PAIRS, 0)
        right_group = lax.dynamic_slice_in_dim(right_ops, first, PAIRS, 0)
        offset_group = lax.dynamic_slice_in_dim(offsets, first, PAIRS, 0)
        vector = lax.dynamic_index_in_dim(vectors, sector, 0, keepdims=False)
        stacked = partials(vector, left_group, right_group, offset_group).astype(jnp.float32)
        current = lax.dynamic_slice_in_dim(accumulated, sector, 3, 0)
        return lax.dynamic_update_slice_in_dim(accumulated, current + stacked, sector, 0), None

    start = jnp.zeros((SECTORS + 2, ROOTS, B, B), jnp.float32)
    accumulated, _ = lax.scan(add_group, start, jnp.arange(groups, dtype=jnp.int32))
    return accumulated[1:-1]


def reference(wavefunction, diagonal, left_ops, right_ops, offsets):
    vectors = wavefunction
    for turn in range(ITERS):
        sigma = apply_sigma(vectors, left_ops, right_ops, offsets)
        vectors = (sigma / diagonal[:, None]).astype(jnp.bfloat16)
    return vectors
```

```python
import jax
import jax.numpy as jnp
from jax import lax
from jax.sharding import PartitionSpec as P

ITERS = 2


def swap(block, axis, distance):
    route = [(i, i ^ distance) for i in range(lax.axis_size(axis))]
    return lax.ppermute(block, axis, route)


def side(axis, distance):
    return lax.rem(lax.axis_index(axis) // distance, 2)


def split(block, distance, rows):
    roots, height, width = block.shape
    return block.reshape(roots, height // (2 * rows), 2, rows, width)


def widen(block, distance, which):
    other = swap(block, "op", distance)
    low = jnp.where(which == 0, block, other)
    high = jnp.where(which == 0, other, block)
    return low, high


def on_device(wavefunction, diagonal, left_ops, right_ops, offsets):
    nothing = jnp.zeros((), jnp.bfloat16)
    raise_mask = (offsets[:, 0] == 1)[:, None, None]
    lower_mask = (offsets[:, 1] == 1)[:, None, None]
    left_raise = jnp.where(raise_mask, left_ops, nothing)
    left_stay = jnp.where(raise_mask, nothing, left_ops)
    left_lower = jnp.where(lower_mask, left_ops, nothing)
    left_back = jnp.where(lower_mask, nothing, left_ops)
    members = lax.axis_size("op")
    sectors = lax.axis_size("sec")
    odd = side("sec", 1) == 1
    steps = [1 << k for k in range(members.bit_length() - 1)]
    roots, shard, width = wavefunction.shape[1:]
    own = diagonal[0]
    last = steps[-1]
    last_side = side("op", last)
    other = swap(own, "op", last)
    both = jnp.stack([jnp.where(last_side == 0, own, other), jnp.where(last_side == 0, other, own)])

    def grow(block, distance):
        which = side("op", distance)
        arrived = swap(block, "op", distance)
        low = jnp.where(which == 0, block, arrived)
        high = jnp.where(which == 0, arrived, block)
        return jnp.stack([low, high], axis=2).reshape(roots, -1, shard, width)

    def gather(block, distances):
        for distance in distances:
            block = grow(block, distance)
        return block

    vector = gather(wavefunction[0][:, None], steps[::-1])
    for turn in range(ITERS):
        rows_block = vector.reshape(roots, members * shard, width)
        turned = jnp.einsum(
            "xab,pcb->pxac", rows_block, right_ops, preferred_element_type=jnp.float32
        ).astype(jnp.bfloat16)
        plain = jnp.einsum(
            "xab,pbc->pxac", rows_block, right_ops, preferred_element_type=jnp.float32
        ).astype(jnp.bfloat16)
        raised = jnp.einsum(
            "pab,pxbc->xac", left_raise, turned, preferred_element_type=jnp.float32
        ).astype(jnp.bfloat16)
        lowered = jnp.einsum(
            "pba,pxbc->xac", left_lower, plain, preferred_element_type=jnp.float32
        ).astype(jnp.bfloat16)
        staying = jnp.einsum(
            "pab,pxbc->xac", left_stay, turned, preferred_element_type=jnp.float32
        )
        staying = staying + jnp.einsum(
            "pba,pxbc->xac", left_back, plain, preferred_element_type=jnp.float32
        )
        staying = staying.astype(jnp.bfloat16)
        near = jnp.where(odd, lowered, raised)
        cross = jnp.where(odd, raised, lowered)
        from_cross = lax.ppermute(
            cross,
            "sec",
            [(i, i + 1) for i in range(1, sectors - 1, 2)] + [(i, i - 1) for i in range(2, sectors, 2)],
        )
        from_near = swap(near, "sec", 1)
        block = (
            staying.astype(jnp.float32) + from_near.astype(jnp.float32) + from_cross.astype(jnp.float32)
        ).astype(jnp.bfloat16)
        block = block.reshape(roots, members, shard, width)
        final = turn == ITERS - 1
        for distance in steps:
            which = side("op", distance)
            if distance == last and not final:
                arrived = swap(block, "op", distance)
                total = block.astype(jnp.float32) + arrived.astype(jnp.float32)
                block = (total / both[None]).astype(jnp.bfloat16)
                break
            halves = block.reshape(roots, -1, 2, shard, width)
            keep = jnp.where(which == 0, halves[:, :, 0], halves[:, :, 1])
            send = jnp.where(which == 0, halves[:, :, 1], halves[:, :, 0])
            arrived = swap(send, "op", distance)
            total = keep.astype(jnp.float32) + arrived.astype(jnp.float32)
            if distance == last:
                return (total[:, 0] / own[None]).astype(jnp.bfloat16)[None]
            block = total.astype(jnp.bfloat16)
        vector = gather(block, steps[-2::-1])


def solution(mesh):
    in_specs = (
        P("sec", None, "op", None),
        P("sec", "op", None),
        P(("sec", "op"), None, None),
        P(("sec", "op"), None, None),
        P(("sec", "op"), None),
    )
    out_specs = P("sec", None, "op", None)
    return jax.shard_map(
        on_device, mesh=mesh, in_specs=in_specs, out_specs=out_specs, check_vma=False
    )
```

```python
import functools

import jax
import jax.numpy as jnp
from jax import lax
from jax.experimental import pallas as pl
from jax.experimental.pallas import tpu as pltpu
from jax.sharding import PartitionSpec as P

ITERS = 2
LIMIT = 32 * 1024 * 1024
COST = 2000000000
VMEM = pl.BlockSpec(memory_space=pltpu.VMEM)
SMEM = pl.BlockSpec(memory_space=pltpu.SMEM)


def swap(block, axis, distance):
    route = [(i, i ^ distance) for i in range(lax.axis_size(axis))]
    return lax.ppermute(block, axis, route)


def side(axis, distance):
    return lax.rem(lax.axis_index(axis) // distance, 2)


def mirrored(index, bits):
    return sum(((index >> k) & 1) << (bits - 1 - k) for k in range(bits))


def outer_slot():
    return 1 - side("sec", 2) if lax.axis_size("sec") == 4 else 0 * lax.axis_index("sec")


def arrange_kernel(slot, own_steps, other_steps, left_own, left_other, right_own, right_other, piece, *outs):
    lefts, rights, counts, passed = outs
    pairs, size, _ = left_own.shape
    own = (side("sec", 1) == outer_slot()) == (slot == 0)
    passed[...] = piece[...]
    for term in range(2):
        moving = [jnp.where(own, own_steps[p, term], other_steps[p, term]) for p in range(pairs)]
        total = functools.reduce(lambda a, b: a + b, moving)
        counts[term] = jnp.full(counts.shape[1:], total, jnp.int32)
        ahead, behind = 0, total
        for p in range(pairs):
            place = jnp.where(moving[p] == 1, ahead, behind)
            ahead, behind = ahead + moving[p], behind + 1 - moving[p]
            columns = pl.ds(pl.multiple_of(place * size, 128), size)
            left = jnp.where(own, left_own[p], left_other[p])
            right = jnp.where(own, right_own[p], right_other[p])
            rights[term, :, columns] = right.T if term == 0 else right
            lefts[term, :, columns] = left if term == 0 else left.T


def arrange(slot, steps, lefts, rights, piece):
    pairs, size, _ = lefts[0].shape
    shape = jax.ShapeDtypeStruct((2, size, pairs * size), lefts[0].dtype)
    counts = jax.ShapeDtypeStruct((2, 8, 128), jnp.int32)
    return pl.pallas_call(
        functools.partial(arrange_kernel, slot),
        out_shape=(shape, shape, counts, jax.ShapeDtypeStruct(piece.shape, piece.dtype)),
        in_specs=[SMEM] * 2 + [VMEM] * 5,
        out_specs=(VMEM,) * 4,
        compiler_params=pltpu.CompilerParams(vmem_limit_bytes=LIMIT),
        cost_estimate=pl.CostEstimate(flops=COST, bytes_accessed=1, transcendentals=0),
        name="arrange",
    )(*steps, *lefts, *rights, piece)


def chunks(size, parts):
    rows = size // parts
    if rows % 16:
        return [(0, 0, size)]
    bits = parts.bit_length() - 1
    return [(i * rows, mirrored(i, bits) * rows, rows) for i in range(parts)]


def put(ref, value, parts):
    for natural, at, rows in chunks(value.shape[0], parts):
        ref[at : at + rows] = value[natural : natural + rows].astype(ref.dtype)


def one_term(parts, term, counts, vector, lefts, rights, middle, moved, stayed):
    size = vector.shape[0]
    pairs = middle.shape[0] // size
    movers = jnp.where(term == 0, jnp.max(counts[0]), jnp.max(counts[1]))
    step = 2 if pairs % 2 == 0 else 1
    for first in range(0, pairs, step):
        columns = slice(first * size, (first + step) * size)
        turned = jnp.dot(vector[...], rights[term, :, columns], preferred_element_type=jnp.float32)
        turned = turned.astype(middle.dtype)
        for p in range(step):
            for natural, at, rows in chunks(size, parts):
                to = (first + p) * size + natural
                middle[to : to + rows] = turned[at : at + rows, p * size : (p + 1) * size]
    for count in range(pairs + 1):

        @pl.when(movers == count)
        def _(cut=count * size):
            def total(part):
                if part.start == part.stop:
                    return None
                return jnp.dot(lefts[term, :, part], middle[part], preferred_element_type=jnp.float32)

            if moved is not None:
                moved(total(slice(0, cut)))
            stayed(total(slice(cut, pairs * size)))


def none_or(total, base):
    if total is None:
        return base
    return total if base is None else total + base


def inner_kernel(parts, with_cross, counts, vector, lefts, rights, near, stayed, *rest):
    cross, middle = rest if with_cross else (None, *rest)
    size = vector.shape[0]
    zeros = functools.partial(jnp.zeros, (size, size), jnp.float32)
    term = outer_slot()

    def set_near(total):
        near[...] = zeros() if total is None else total

    def set_stayed(total):
        stayed[...] = zeros() if total is None else total

    def set_cross(total):
        put(cross, zeros() if total is None else total, parts)

    def add_stayed(total):
        if total is not None:
            stayed[...] += total

    one_term(parts, 1 - term, counts, vector, lefts, rights, middle, set_near, set_stayed)
    one_term(
        parts, term, counts, vector, lefts, rights, middle, set_cross if with_cross else None, add_stayed
    )


def first_kernel(parts, counts, vector, lefts, rights, cross, stayed, middle):
    size = vector.shape[0]
    zeros = functools.partial(jnp.zeros, (size, size), jnp.float32)

    def set_cross(total):
        put(cross, zeros() if total is None else total, parts)

    def set_stayed(total):
        stayed[...] = zeros() if total is None else total

    one_term(parts, 1 - outer_slot(), counts, vector, lefts, rights, middle, set_cross, set_stayed)


def second_kernel(parts, counts, vector, lefts, rights, stayed, near_in, stayed_in, own, other, middle):
    def set_other(total):
        put(other, none_or(total, stayed_in[...]), parts)

    def set_own(total):
        put(own, none_or(total, stayed[...] + near_in[...]), parts)

    one_term(parts, outer_slot(), counts, vector, lefts, rights, middle, set_other, set_own)


def merge_kernel(own, arrived, other, *rest):
    more, outer, inner = rest if len(rest) == 3 else (None, *rest)
    outer[...] = (own[...] + arrived[...].astype(jnp.float32)).astype(outer.dtype)
    total = other[...]
    if more is not None:
        total = total + more[...].astype(jnp.float32)
    inner[...] = total.astype(inner.dtype)


def merge(own, arrived, other, *more):
    shape = jax.ShapeDtypeStruct(own.shape, jnp.bfloat16)
    return pl.pallas_call(
        merge_kernel,
        out_shape=(shape, shape),
        in_specs=[VMEM] * (3 + len(more)),
        out_specs=(VMEM, VMEM),
        compiler_params=pltpu.CompilerParams(vmem_limit_bytes=LIMIT),
        cost_estimate=pl.CostEstimate(flops=1, bytes_accessed=1, transcendentals=0),
        name="merge",
    )(own, arrived, other, *more)


def call(kernel, name, kinds, cost, vector, weights, *more):
    lefts, rights, counts = weights
    size, width = lefts.shape[1:]
    shapes = tuple(jax.ShapeDtypeStruct((size, size), kind) for kind in kinds)
    return pl.pallas_call(
        kernel,
        out_shape=shapes,
        in_specs=[VMEM] * (4 + len(more)),
        out_specs=(VMEM,) * len(shapes),
        scratch_shapes=[pltpu.VMEM((width, size), jnp.bfloat16)],
        compiler_params=pltpu.CompilerParams(vmem_limit_bytes=LIMIT),
        cost_estimate=pl.CostEstimate(flops=cost, bytes_accessed=1, transcendentals=0),
        name=name,
    )(counts, vector, lefts, rights, *more)


def on_device(wavefunction, diagonal, left_ops, right_ops, offsets):
    members = lax.axis_size("op")
    sectors = lax.axis_size("sec")
    bits = members.bit_length() - 1
    steps = [1 << k for k in range(bits)]
    groups, last = [steps[k : min(k + 2, bits - 1)] for k in range(0, bits - 1, 2)], steps[-1]
    sides = {d: side("op", d) for d in steps}
    shard, width = wavefunction.shape[2:]
    size = members * shard
    core = side("sec", 1)
    bf16, f32 = jnp.bfloat16, jnp.float32
    pair = sectors == 4
    mine = core == outer_slot()

    def both_slots(own, other):
        return jnp.where(mine, own, other), jnp.where(mine, other, own)

    def position(group):
        return functools.reduce(lambda a, d: 2 * a + sides[d], group, 0)

    def partners(group):
        count = 1 << len(group)
        return [(j, sum(d for k, d in enumerate(group) if j >> (len(group) - 1 - k) & 1)) for j in range(count - 1, 0, -1)]

    def scatter(block, group):
        rows = block.shape[0] >> len(group)
        place = position(group)
        sent = [lax.dynamic_slice_in_dim(block, (place ^ j) * rows, rows) for j, _ in partners(group)]
        arrived = [swap(piece, "op", distance) for piece, (_, distance) in zip(sent, partners(group))]
        total = lax.dynamic_slice_in_dim(block, place * rows, rows).astype(f32)
        for piece in arrived:
            total = total + piece.astype(f32)
        return total

    def gather(block, group, own=None):
        rows = block.shape[0]
        place = position(group)
        whole = jnp.zeros((rows << len(group), block.shape[1]), block.dtype)
        whole = lax.dynamic_update_slice_in_dim(whole, block if own is None else own, place * rows, 0)
        for j, distance in partners(group):
            whole = lax.dynamic_update_slice_in_dim(whole, swap(block, "op", distance), (place ^ j) * rows, 0)
        return whole

    def respread(block):
        if shard % 16 == 0:
            return block
        spread = block.reshape((2,) * bits + (shard, -1))
        return spread.transpose(tuple(range(bits))[::-1] + (bits, bits + 1)).reshape(block.shape)

    def gather_all(block):
        for group in groups[::-1]:
            block = gather(block, group)
        return respread(block)

    def beside(block, own=None):
        own = block if own is None else own
        arrived = swap(block, "op", last)
        low = jnp.where(sides[last] == 0, own, arrived)
        high = jnp.where(sides[last] == 0, arrived, own)
        return jnp.concatenate([low, high])

    own_roots = wavefunction[0]
    other_roots = swap(own_roots, "sec", 1)
    lefts = (left_ops, swap(left_ops, "sec", 1))
    rights = (right_ops, swap(right_ops, "sec", 1))
    moves = (offsets, swap(offsets, "sec", 1))
    own_root = jnp.where(core == 0, own_roots[0], own_roots[1])
    other_root = jnp.where(core == 0, other_roots[0], other_roots[1])
    start = jnp.concatenate(both_slots(own_root, other_root), axis=1)
    *outer_weights, passed = arrange(0, moves, lefts, rights, start)
    together = beside(start, passed)
    *inner_weights, passed = arrange(1, moves, lefts, rights, together)
    together = gather(together, groups[-1], passed)
    for group in groups[-2::-1]:
        together = gather(together, group)
    together = respread(together)
    vectors = [together[:, :width], together[:, width:]]
    own_diagonals = both_slots(diagonal[0], swap(diagonal[0], "sec", 1))
    both_diagonals = beside(jnp.concatenate(own_diagonals, axis=1))
    diagonals = [both_diagonals[:, :width], both_diagonals[:, width:]]

    for turn in range(ITERS):
        cross, stayed = call(
            functools.partial(first_kernel, members), "first", (bf16, f32), COST, vectors[0], outer_weights
        )
        kinds = (f32, f32) if pair else (f32, f32, bf16)
        inner = call(functools.partial(inner_kernel, members, not pair), "inner", kinds, COST, vectors[1], inner_weights)
        if pair:
            arrived = (swap(respread(cross), "sec", 2),)
        else:
            arrived = (
                lax.ppermute(respread(inner[2]), "sec", [(i, i + 2) for i in range(sectors - 2)]),
                lax.ppermute(respread(cross), "sec", [(i, i - 2) for i in range(2, sectors)]),
            )
        own, other = call(
            functools.partial(second_kernel, members),
            "second",
            (f32, f32),
            COST,
            vectors[0],
            outer_weights,
            stayed,
            inner[0],
            inner[1],
        )
        blocks = list(merge(respread(own), arrived[0], respread(other), *arrived[1:]))
        for k in range(2):
            block = blocks[k]
            for group in groups:
                block = scatter(block, group).astype(bf16)
            if turn < ITERS - 1:
                total = block.astype(f32) + swap(block, "op", last).astype(f32)
                vectors[k] = gather_all((total / diagonals[k]).astype(bf16))
            else:
                blocks[k] = (scatter(block, [last]) / own_diagonals[k]).astype(bf16)
    kept = jnp.where(mine, blocks[0], blocks[1])
    returned = swap(jnp.where(mine, blocks[1], blocks[0]), "sec", 1)
    out = jnp.where(core == 0, jnp.stack([kept, returned]), jnp.stack([returned, kept]))
    return out[None]


def solution(mesh):
    in_specs = (
        P("sec", None, "op", None),
        P("sec", "op", None),
        P(("sec", "op"), None, None),
        P(("sec", "op"), None, None),
        P(("sec", "op"), None),
    )
    out_specs = P("sec", None, "op", None)
    return jax.shard_map(
        on_device, mesh=mesh, in_specs=in_specs, out_specs=out_specs, check_vma=False
    )
```

```python
import functools

import jax
import jax.numpy as jnp
from jax import lax
from jax.experimental import pallas as pl
from jax.experimental.pallas import tpu as pltpu
from jax.sharding import PartitionSpec as P

ITERS = 2
LIMIT = 32 * 1024 * 1024
COST = 5 * 10**9
VMEM = pl.BlockSpec(memory_space=pltpu.VMEM)
SMEM = pl.BlockSpec(memory_space=pltpu.SMEM)


def swap(block, axis, distance):
    route = [(i, i ^ distance) for i in range(lax.axis_size(axis))]
    return lax.ppermute(block, axis, route)


def side(axis, distance):
    return lax.rem(lax.axis_index(axis) // distance, 2)


def mirrored(index, bits):
    return sum(((index >> k) & 1) << (bits - 1 - k) for k in range(bits))


def outer_slot():
    return 1 - side("sec", 2) if lax.axis_size("sec") == 4 else 0 * lax.axis_index("sec")


def arrange_kernel(slot, own_steps, other_steps, left_own, left_other, right_own, right_other, *rest):
    *pieces, lefts, rights, counts, passed = rest
    pairs, size, _ = left_own.shape
    own_first = side("sec", 1) == outer_slot()
    own = own_first == (slot == 0)
    if len(pieces) == 1:
        passed[...] = pieces[0][...]
    else:
        width = pieces[0].shape[1]
        passed[:, :width] = jnp.where(own_first, pieces[0][...], pieces[1][...])
        passed[:, width:] = jnp.where(own_first, pieces[1][...], pieces[0][...])
    for term in range(2):
        moving = [jnp.where(own, own_steps[p, term], other_steps[p, term]) for p in range(pairs)]
        total = functools.reduce(lambda a, b: a + b, moving)
        counts[term] = jnp.full(counts.shape[1:], total, jnp.int32)
        ahead, behind = 0, total
        for p in range(pairs):
            place = jnp.where(moving[p] == 1, ahead, behind)
            ahead, behind = ahead + moving[p], behind + 1 - moving[p]
            columns = pl.ds(pl.multiple_of(place * size, 128), size)
            left = jnp.where(own, left_own[p], left_other[p])
            right = jnp.where(own, right_own[p], right_other[p])
            rights[term, :, columns] = right.T if term == 0 else right
            lefts[term, :, columns] = left if term == 0 else left.T


def arrange(slot, steps, lefts, rights, *pieces):
    pairs, size, _ = lefts[0].shape
    rows, width = pieces[0].shape
    shape = jax.ShapeDtypeStruct((2, size, pairs * size), lefts[0].dtype)
    counts = jax.ShapeDtypeStruct((2, 8, 128), jnp.int32)
    return pl.pallas_call(
        functools.partial(arrange_kernel, slot),
        out_shape=(shape, shape, counts, jax.ShapeDtypeStruct((rows, width * len(pieces)), pieces[0].dtype)),
        in_specs=[SMEM] * 2 + [VMEM] * (4 + len(pieces)),
        out_specs=(VMEM,) * 4,
        compiler_params=pltpu.CompilerParams(vmem_limit_bytes=LIMIT),
        cost_estimate=pl.CostEstimate(flops=COST, bytes_accessed=1, transcendentals=0),
        name="arrange",
    )(*steps, *lefts, *rights, *pieces)


def chunks(size, parts):
    rows = size // parts
    if rows % 16:
        return [(0, 0, size)]
    bits = parts.bit_length() - 1
    return [(i * rows, mirrored(i, bits) * rows, rows) for i in range(parts)]


def put(ref, value, parts):
    for natural, at, rows in chunks(value.shape[0], parts):
        ref[at : at + rows] = value[natural : natural + rows].astype(ref.dtype)


def one_term(parts, term, counts, vector, lefts, rights, middle, moved, stayed):
    size = vector.shape[0]
    pairs = middle.shape[0] // size
    movers = jnp.where(term == 0, jnp.max(counts[0]), jnp.max(counts[1]))
    step = 2 if pairs % 2 == 0 else 1
    for first in range(0, pairs, step):
        columns = slice(first * size, (first + step) * size)
        turned = jnp.dot(vector[...], rights[term, :, columns], preferred_element_type=jnp.float32)
        turned = turned.astype(middle.dtype)
        for p in range(step):
            for natural, at, rows in chunks(size, parts):
                to = (first + p) * size + natural
                middle[to : to + rows] = turned[at : at + rows, p * size : (p + 1) * size]
    for count in range(pairs + 1):

        @pl.when(movers == count)
        def _(cut=count * size):
            def total(part):
                if part.start == part.stop:
                    return None
                return jnp.dot(lefts[term, :, part], middle[part], preferred_element_type=jnp.float32)

            if moved is not None:
                moved(total(slice(0, cut)))
            stayed(total(slice(cut, pairs * size)))


def none_or(total, base):
    if total is None:
        return base
    return total if base is None else total + base


def inner_kernel(parts, with_cross, counts, vector, lefts, rights, near, stayed, *rest):
    cross, middle = rest if with_cross else (None, *rest)
    size = vector.shape[0]
    zeros = functools.partial(jnp.zeros, (size, size), jnp.float32)
    term = outer_slot()

    def set_near(total):
        near[...] = zeros() if total is None else total

    def set_stayed(total):
        stayed[...] = zeros() if total is None else total

    def set_cross(total):
        put(cross, zeros() if total is None else total, parts)

    def add_stayed(total):
        if total is not None:
            stayed[...] += total

    one_term(parts, 1 - term, counts, vector, lefts, rights, middle, set_near, set_stayed)
    one_term(
        parts, term, counts, vector, lefts, rights, middle, set_cross if with_cross else None, add_stayed
    )


def first_kernel(parts, counts, vector, lefts, rights, cross, stayed, middle):
    size = vector.shape[0]
    zeros = functools.partial(jnp.zeros, (size, size), jnp.float32)

    def set_cross(total):
        put(cross, zeros() if total is None else total, parts)

    def set_stayed(total):
        stayed[...] = zeros() if total is None else total

    one_term(parts, 1 - outer_slot(), counts, vector, lefts, rights, middle, set_cross, set_stayed)


def second_kernel(parts, counts, vector, lefts, rights, stayed, near_in, stayed_in, own, other, middle):
    def set_other(total):
        put(other, none_or(total, stayed_in[...]), parts)

    def set_own(total):
        put(own, none_or(total, stayed[...] + near_in[...]), parts)

    one_term(parts, outer_slot(), counts, vector, lefts, rights, middle, set_other, set_own)


def merge_kernel(own, arrived, other, *rest):
    more, outer, inner = rest if len(rest) == 3 else (None, *rest)
    outer[...] = (own[...] + arrived[...].astype(jnp.float32)).astype(outer.dtype)
    total = other[...]
    if more is not None:
        total = total + more[...].astype(jnp.float32)
    inner[...] = total.astype(inner.dtype)


def merge(own, arrived, other, *more):
    shape = jax.ShapeDtypeStruct(own.shape, jnp.bfloat16)
    return pl.pallas_call(
        merge_kernel,
        out_shape=(shape, shape),
        in_specs=[VMEM] * (3 + len(more)),
        out_specs=(VMEM, VMEM),
        compiler_params=pltpu.CompilerParams(vmem_limit_bytes=LIMIT),
        cost_estimate=pl.CostEstimate(flops=1, bytes_accessed=1, transcendentals=0),
        name="merge",
    )(own, arrived, other, *more)


def call(kernel, name, kinds, cost, vector, weights, *more):
    lefts, rights, counts = weights
    size, width = lefts.shape[1:]
    shapes = tuple(jax.ShapeDtypeStruct((size, size), kind) for kind in kinds)
    return pl.pallas_call(
        kernel,
        out_shape=shapes,
        in_specs=[VMEM] * (4 + len(more)),
        out_specs=(VMEM,) * len(shapes),
        scratch_shapes=[pltpu.VMEM((width, size), jnp.bfloat16)],
        compiler_params=pltpu.CompilerParams(vmem_limit_bytes=LIMIT),
        cost_estimate=pl.CostEstimate(flops=cost, bytes_accessed=1, transcendentals=0),
        name=name,
    )(counts, vector, lefts, rights, *more)


def on_device(wavefunction, diagonal, left_ops, right_ops, offsets):
    members = lax.axis_size("op")
    sectors = lax.axis_size("sec")
    bits = members.bit_length() - 1
    steps = [1 << k for k in range(bits)]
    groups, last = [steps[k : min(k + 2, bits - 1)] for k in range(0, bits - 1, 2)], steps[-1]
    sides = {d: side("op", d) for d in steps}
    shard, width = wavefunction.shape[2:]
    size = members * shard
    core = side("sec", 1)
    bf16, f32 = jnp.bfloat16, jnp.float32
    pair = sectors == 4
    mine = core == outer_slot()

    def both_slots(own, other):
        return jnp.where(mine, own, other), jnp.where(mine, other, own)

    def position(group):
        return functools.reduce(lambda a, d: 2 * a + sides[d], group, 0)

    def partners(group):
        count = 1 << len(group)
        return [(j, sum(d for k, d in enumerate(group) if j >> (len(group) - 1 - k) & 1)) for j in range(count - 1, 0, -1)]

    def scatter(block, group):
        rows = block.shape[0] >> len(group)
        place = position(group)
        sent = [lax.dynamic_slice_in_dim(block, (place ^ j) * rows, rows) for j, _ in partners(group)]
        arrived = [swap(piece, "op", distance) for piece, (_, distance) in zip(sent, partners(group))]
        total = lax.dynamic_slice_in_dim(block, place * rows, rows).astype(f32)
        for piece in arrived:
            total = total + piece.astype(f32)
        return total

    def gather(block, group, own=None):
        rows = block.shape[0]
        place = position(group)
        whole = jnp.zeros((rows << len(group), block.shape[1]), block.dtype)
        whole = lax.dynamic_update_slice_in_dim(whole, block if own is None else own, place * rows, 0)
        for j, distance in partners(group):
            whole = lax.dynamic_update_slice_in_dim(whole, swap(block, "op", distance), (place ^ j) * rows, 0)
        return whole

    def respread(block):
        if shard % 16 == 0:
            return block
        spread = block.reshape((2,) * bits + (shard, -1))
        return spread.transpose(tuple(range(bits))[::-1] + (bits, bits + 1)).reshape(block.shape)

    def gather_all(block):
        for group in groups[::-1]:
            block = gather(block, group)
        return respread(block)

    def beside(block, own=None):
        own = block if own is None else own
        arrived = swap(block, "op", last)
        low = jnp.where(sides[last] == 0, own, arrived)
        high = jnp.where(sides[last] == 0, arrived, own)
        return jnp.concatenate([low, high])

    own_roots = wavefunction[0]
    other_roots = swap(own_roots, "sec", 1)
    own_root = jnp.where(core == 0, own_roots[0], own_roots[1])
    other_root = jnp.where(core == 0, other_roots[0], other_roots[1])
    start = jnp.concatenate(both_slots(own_root, other_root), axis=1)
    start, left_given, right_given = lax.optimization_barrier((start, left_ops, right_ops))
    lefts = (left_ops, swap(left_given, "sec", 1))
    rights = (right_ops, swap(right_given, "sec", 1))
    moves = (offsets, swap(offsets, "sec", 1))
    *outer_weights, passed = arrange(0, moves, lefts, rights, start)
    together = beside(start, passed)
    vectors = [gather_all(together[:, :width]), gather_all(together[:, width:])]
    own_diagonal = diagonal[0]
    *inner_weights, slots = arrange(1, moves, lefts, rights, own_diagonal, swap(own_diagonal, "sec", 1))
    both_diagonals = beside(slots)
    own_diagonals = [slots[:, :width], slots[:, width:]]
    diagonals = [both_diagonals[:, :width], both_diagonals[:, width:]]

    for turn in range(ITERS):
        cross, stayed = call(
            functools.partial(first_kernel, members), "first", (bf16, f32), COST, vectors[0], outer_weights
        )
        kinds = (f32, f32) if pair else (f32, f32, bf16)
        inner = call(functools.partial(inner_kernel, members, not pair), "inner", kinds, COST, vectors[1], inner_weights)
        if pair:
            arrived = (swap(respread(cross), "sec", 2),)
        else:
            arrived = (
                lax.ppermute(respread(inner[2]), "sec", [(i, i + 2) for i in range(sectors - 2)]),
                lax.ppermute(respread(cross), "sec", [(i, i - 2) for i in range(2, sectors)]),
            )
        own, other = call(
            functools.partial(second_kernel, members),
            "second",
            (f32, f32),
            COST,
            vectors[0],
            outer_weights,
            stayed,
            inner[0],
            inner[1],
        )
        blocks = list(merge(respread(own), arrived[0], respread(other), *arrived[1:]))
        for k in (0, 1):
            block = blocks[k]
            for group in groups:
                block = scatter(block, group).astype(bf16)
            if turn < ITERS - 1:
                total = block.astype(f32) + swap(block, "op", last).astype(f32)
                vectors[k] = gather_all((total / diagonals[k]).astype(bf16))
            else:
                blocks[k] = (scatter(block, [last]) / own_diagonals[k]).astype(bf16)
    kept = jnp.where(mine, blocks[0], blocks[1])
    returned = swap(jnp.where(mine, blocks[1], blocks[0]), "sec", 1)
    out = jnp.where(core == 0, jnp.stack([kept, returned]), jnp.stack([returned, kept]))
    return out[None]


def solution(mesh):
    in_specs = (
        P("sec", None, "op", None),
        P("sec", "op", None),
        P(("sec", "op"), None, None),
        P(("sec", "op"), None, None),
        P(("sec", "op"), None),
    )
    out_specs = P("sec", None, "op", None)
    return jax.shard_map(
        on_device, mesh=mesh, in_specs=in_specs, out_specs=out_specs, check_vma=False
    )
```

```python
import functools

import jax
import jax.numpy as jnp
from jax import lax
from jax.experimental import pallas as pl
from jax.experimental.pallas import tpu as pltpu
from jax.sharding import PartitionSpec as P

ITERS = 2
LIMIT = 8 * 1024 * 1024
COST = 5 * 10**9
VMEM = pl.BlockSpec(memory_space=pltpu.VMEM)
SMEM = pl.BlockSpec(memory_space=pltpu.SMEM)


def swap(block, axis, distance):
    route = [(i, i ^ distance) for i in range(lax.axis_size(axis))]
    return lax.ppermute(block, axis, route)


def side(axis, distance):
    return lax.rem(lax.axis_index(axis) // distance, 2)


def mirrored(index, bits):
    return sum(((index >> k) & 1) << (bits - 1 - k) for k in range(bits))


def outer_slot():
    return 1 - side("sec", 2) if lax.axis_size("sec") == 4 else 0 * lax.axis_index("sec")


def arrange_kernel(slot, own_steps, other_steps, left_own, left_other, right_own, right_other, *rest):
    *pieces, lefts, rights, counts, passed = rest
    pairs, size, _ = left_own.shape
    own_first = side("sec", 1) == outer_slot()
    own = own_first == (slot == 0)
    if len(pieces) == 1:
        passed[...] = pieces[0][...]
    else:
        width = pieces[0].shape[1]
        passed[:, :width] = jnp.where(own_first, pieces[0][...], pieces[1][...])
        passed[:, width:] = jnp.where(own_first, pieces[1][...], pieces[0][...])
    for term in range(2):
        moving = [jnp.where(own, own_steps[p, term], other_steps[p, term]) for p in range(pairs)]
        total = functools.reduce(lambda a, b: a + b, moving)
        counts[term] = jnp.full(counts.shape[1:], total, jnp.int32)
        ahead, behind = 0, total
        for p in range(pairs):
            place = jnp.where(moving[p] == 1, ahead, behind)
            ahead, behind = ahead + moving[p], behind + 1 - moving[p]
            columns = pl.ds(pl.multiple_of(place * size, 128), size)
            left = jnp.where(own, left_own[p], left_other[p])
            right = jnp.where(own, right_own[p], right_other[p])
            rights[term, :, columns] = right.T if term == 0 else right
            lefts[term, :, columns] = left if term == 0 else left.T


def arrange(slot, steps, lefts, rights, *pieces):
    pairs, size, _ = lefts[0].shape
    rows, width = pieces[0].shape
    shape = jax.ShapeDtypeStruct((2, size, pairs * size), lefts[0].dtype)
    counts = jax.ShapeDtypeStruct((2, 8, 128), jnp.int32)
    return pl.pallas_call(
        functools.partial(arrange_kernel, slot),
        out_shape=(shape, shape, counts, jax.ShapeDtypeStruct((rows, width * len(pieces)), pieces[0].dtype)),
        in_specs=[SMEM] * 2 + [VMEM] * (4 + len(pieces)),
        out_specs=(VMEM,) * 4,
        compiler_params=pltpu.CompilerParams(vmem_limit_bytes=LIMIT),
        cost_estimate=pl.CostEstimate(flops=COST, bytes_accessed=1, transcendentals=0),
        name="arrange",
    )(*steps, *lefts, *rights, *pieces)


def chunks(size, parts):
    rows = size // parts
    if rows % 16:
        return [(0, 0, size)]
    bits = parts.bit_length() - 1
    return [(i * rows, mirrored(i, bits) * rows, rows) for i in range(parts)]


def put(ref, value, parts):
    for natural, at, rows in chunks(value.shape[0], parts):
        ref[at : at + rows] = value[natural : natural + rows].astype(ref.dtype)


def one_term(parts, term, counts, vector, lefts, rights, middle, moved, stayed):
    size = vector.shape[0]
    pairs = middle.shape[0] // size
    movers = jnp.where(term == 0, jnp.max(counts[0]), jnp.max(counts[1]))
    step = 2 if pairs % 2 == 0 else 1
    for first in range(0, pairs, step):
        columns = slice(first * size, (first + step) * size)
        turned = jnp.dot(vector[...], rights[term, :, columns], preferred_element_type=jnp.float32)
        turned = turned.astype(middle.dtype)
        for p in range(step):
            for natural, at, rows in chunks(size, parts):
                to = (first + p) * size + natural
                middle[to : to + rows] = turned[at : at + rows, p * size : (p + 1) * size]
    for count in range(pairs + 1):

        @pl.when(movers == count)
        def _(cut=count * size):
            def total(part):
                if part.start == part.stop:
                    return None
                return jnp.dot(lefts[term, :, part], middle[part], preferred_element_type=jnp.float32)

            if moved is not None:
                moved(total(slice(0, cut)))
            stayed(total(slice(cut, pairs * size)))


def none_or(total, base):
    if total is None:
        return base
    return total if base is None else total + base


def inner_kernel(parts, with_cross, counts, vector, lefts, rights, near, stayed, *rest):
    cross, middle = rest if with_cross else (None, *rest)
    size = vector.shape[0]
    zeros = functools.partial(jnp.zeros, (size, size), jnp.float32)
    term = outer_slot()

    def set_near(total):
        near[...] = zeros() if total is None else total

    def set_stayed(total):
        stayed[...] = zeros() if total is None else total

    def set_cross(total):
        put(cross, zeros() if total is None else total, parts)

    def add_stayed(total):
        if total is not None:
            stayed[...] += total

    one_term(parts, 1 - term, counts, vector, lefts, rights, middle, set_near, set_stayed)
    one_term(
        parts, term, counts, vector, lefts, rights, middle, set_cross if with_cross else None, add_stayed
    )


def first_kernel(parts, counts, vector, lefts, rights, cross, stayed, middle):
    size = vector.shape[0]
    zeros = functools.partial(jnp.zeros, (size, size), jnp.float32)

    def set_cross(total):
        put(cross, zeros() if total is None else total, parts)

    def set_stayed(total):
        stayed[...] = zeros() if total is None else total

    one_term(parts, 1 - outer_slot(), counts, vector, lefts, rights, middle, set_cross, set_stayed)


def second_kernel(parts, counts, vector, lefts, rights, stayed, near_in, stayed_in, own, other, middle):
    def set_other(total):
        put(other, none_or(total, stayed_in[...]), parts)

    def set_own(total):
        put(own, none_or(total, stayed[...] + near_in[...]), parts)

    one_term(parts, outer_slot(), counts, vector, lefts, rights, middle, set_other, set_own)


def merge_kernel(own, arrived, other, *rest):
    more, outer, inner = rest if len(rest) == 3 else (None, *rest)
    outer[...] = (own[...] + arrived[...].astype(jnp.float32)).astype(outer.dtype)
    total = other[...]
    if more is not None:
        total = total + more[...].astype(jnp.float32)
    inner[...] = total.astype(inner.dtype)


def merge(own, arrived, other, *more):
    shape = jax.ShapeDtypeStruct(own.shape, jnp.bfloat16)
    return pl.pallas_call(
        merge_kernel,
        out_shape=(shape, shape),
        in_specs=[VMEM] * (3 + len(more)),
        out_specs=(VMEM, VMEM),
        compiler_params=pltpu.CompilerParams(vmem_limit_bytes=LIMIT),
        cost_estimate=pl.CostEstimate(flops=1, bytes_accessed=1, transcendentals=0),
        name="merge",
    )(own, arrived, other, *more)


def call(kernel, name, kinds, cost, vector, weights, *more):
    lefts, rights, counts = weights
    size, width = lefts.shape[1:]
    shapes = tuple(jax.ShapeDtypeStruct((size, size), kind) for kind in kinds)
    return pl.pallas_call(
        kernel,
        out_shape=shapes,
        in_specs=[VMEM] * (4 + len(more)),
        out_specs=(VMEM,) * len(shapes),
        scratch_shapes=[pltpu.VMEM((width, size), jnp.bfloat16)],
        compiler_params=pltpu.CompilerParams(vmem_limit_bytes=LIMIT),
        cost_estimate=pl.CostEstimate(flops=cost, bytes_accessed=1, transcendentals=0),
        name=name,
    )(counts, vector, lefts, rights, *more)


def on_device(wavefunction, diagonal, left_ops, right_ops, offsets):
    members = lax.axis_size("op")
    sectors = lax.axis_size("sec")
    bits = members.bit_length() - 1
    steps = [1 << k for k in range(bits)]
    groups, last = [steps[k : min(k + 2, bits - 1)] for k in range(0, bits - 1, 2)], steps[-1]
    sides = {d: side("op", d) for d in steps}
    shard, width = wavefunction.shape[2:]
    size = members * shard
    core = side("sec", 1)
    bf16, f32 = jnp.bfloat16, jnp.float32
    pair = sectors == 4
    mine = core == outer_slot()

    def both_slots(own, other):
        return jnp.where(mine, own, other), jnp.where(mine, other, own)

    def position(group):
        return functools.reduce(lambda a, d: 2 * a + sides[d], group, 0)

    def partners(group):
        count = 1 << len(group)
        return [(j, sum(d for k, d in enumerate(group) if j >> (len(group) - 1 - k) & 1)) for j in range(count - 1, 0, -1)]

    def scatter(block, group):
        rows = block.shape[0] >> len(group)
        place = position(group)
        sent = [lax.dynamic_slice_in_dim(block, (place ^ j) * rows, rows) for j, _ in partners(group)]
        arrived = [swap(piece, "op", distance) for piece, (_, distance) in zip(sent, partners(group))]
        total = lax.dynamic_slice_in_dim(block, place * rows, rows).astype(f32)
        for piece in arrived:
            total = total + piece.astype(f32)
        return total

    def gather(block, group, own=None):
        rows = block.shape[0]
        place = position(group)
        first_arrived = None
        whole = jnp.zeros((rows << len(group), block.shape[1]), block.dtype)
        whole = lax.dynamic_update_slice_in_dim(whole, block if own is None else own, place * rows, 0)
        for j, distance in partners(group):
            piece = swap(block, "op", distance)
            first_arrived = piece if first_arrived is None else first_arrived
            whole = lax.dynamic_update_slice_in_dim(whole, piece, (place ^ j) * rows, 0)
        return whole, first_arrived

    def respread(block):
        if shard % 16 == 0:
            return block
        spread = block.reshape((2,) * bits + (shard, -1))
        return spread.transpose(tuple(range(bits))[::-1] + (bits, bits + 1)).reshape(block.shape)

    def gather_all(block):
        for group in groups[::-1]:
            block, first_arrived = gather(block, group)
        return respread(block), first_arrived

    def beside(block, own=None):
        own = block if own is None else own
        arrived = swap(block, "op", last)
        low = jnp.where(sides[last] == 0, own, arrived)
        high = jnp.where(sides[last] == 0, arrived, own)
        return jnp.concatenate([low, high])

    own_roots = wavefunction[0]
    other_roots = swap(own_roots, "sec", 1)
    own_root = jnp.where(core == 0, own_roots[0], own_roots[1])
    other_root = jnp.where(core == 0, other_roots[0], other_roots[1])
    start = jnp.concatenate(both_slots(own_root, other_root), axis=1)
    start, left_given, right_given = lax.optimization_barrier((start, left_ops, right_ops))
    lefts = (left_ops, swap(left_given, "sec", 1))
    rights = (right_ops, swap(right_given, "sec", 1))
    moves = (offsets, swap(offsets, "sec", 1))
    *outer_weights, passed = arrange(0, moves, lefts, rights, start)
    together = beside(start, passed)
    vectors = [gather_all(together[:, :width])[0], gather_all(together[:, width:])[0]]
    own_diagonal = diagonal[0]
    *inner_weights, slots = arrange(1, moves, lefts, rights, own_diagonal, swap(own_diagonal, "sec", 1))
    both_diagonals = beside(slots)
    own_diagonals = [slots[:, :width], slots[:, width:]]
    diagonals = [both_diagonals[:, :width], both_diagonals[:, width:]]

    for turn in range(ITERS):
        cross, stayed = call(
            functools.partial(first_kernel, members), "first", (bf16, f32), COST, vectors[0], outer_weights
        )
        kinds = (f32, f32) if pair else (f32, f32, bf16)
        inner = call(functools.partial(inner_kernel, members, not pair), "inner", kinds, COST, vectors[1], inner_weights)
        if pair:
            arrived = (swap(respread(cross), "sec", 2),)
        else:
            arrived = (
                lax.ppermute(respread(inner[2]), "sec", [(i, i + 2) for i in range(sectors - 2)]),
                lax.ppermute(respread(cross), "sec", [(i, i - 2) for i in range(2, sectors)]),
            )
        own, other = call(
            functools.partial(second_kernel, members),
            "second",
            (f32, f32),
            COST//10,
            vectors[0],
            outer_weights,
            stayed,
            inner[0],
            inner[1],
        )
        blocks = list(merge(respread(own), arrived[0], respread(other), *arrived[1:]))
        for k in (0, 1):
            block = blocks[k]
            for group in groups:
                block = scatter(block, group).astype(bf16)
            if turn < ITERS - 1:
                total = block.astype(f32) + swap(block, "op", last).astype(f32)
                ready = (total / diagonals[k]).astype(bf16)
                if k == 1:
                    ready, _ = lax.optimization_barrier((ready, first_arrived))
                vectors[k], first_arrived = gather_all(ready)
            else:
                blocks[k] = (scatter(block, [last]) / own_diagonals[k]).astype(bf16)
    kept = jnp.where(mine, blocks[0], blocks[1])
    returned = swap(jnp.where(mine, blocks[1], blocks[0]), "sec", 1)
    out = jnp.where(core == 0, jnp.stack([kept, returned]), jnp.stack([returned, kept]))
    return out[None]


def solution(mesh):
    in_specs = (
        P("sec", None, "op", None),
        P("sec", "op", None),
        P(("sec", "op"), None, None),
        P(("sec", "op"), None, None),
        P(("sec", "op"), None),
    )
    out_specs = P("sec", None, "op", None)
    return jax.shard_map(
        on_device, mesh=mesh, in_specs=in_specs, out_specs=out_specs, check_vma=False
    )
```

```python
import functools

import jax
import jax.numpy as jnp
from jax import lax
from jax.experimental import pallas as pl
from jax.experimental.pallas import tpu as pltpu
from jax.sharding import PartitionSpec as P

ITERS = 2
LIMIT = 8 * 1024 * 1024
COST = 5 * 10**9
VMEM = pl.BlockSpec(memory_space=pltpu.VMEM)
SMEM = pl.BlockSpec(memory_space=pltpu.SMEM)


def swap(block, axis, distance):
    route = [(i, i ^ distance) for i in range(lax.axis_size(axis))]
    return lax.ppermute(block, axis, route)


def side(axis, distance):
    return lax.rem(lax.axis_index(axis) // distance, 2)


def mirrored(index, bits):
    return sum(((index >> k) & 1) << (bits - 1 - k) for k in range(bits))


def outer_slot():
    return 1 - side("sec", 2) if lax.axis_size("sec") == 4 else 0 * lax.axis_index("sec")


def arrange_kernel(slot, own_steps, other_steps, left_own, left_other, right_own, right_other, *rest):
    *pieces, lefts, rights, counts, passed = rest
    pairs, size, _ = left_own.shape
    own_first = side("sec", 1) == outer_slot()
    own = own_first == (slot == 0)
    if len(pieces) == 1:
        passed[...] = pieces[0][...]
    else:
        width = pieces[0].shape[1]
        passed[:, :width] = jnp.where(own_first, pieces[0][...], pieces[1][...])
        passed[:, width:] = jnp.where(own_first, pieces[1][...], pieces[0][...])
    for term in range(2):
        moving = [jnp.where(own, own_steps[p, term], other_steps[p, term]) for p in range(pairs)]
        total = functools.reduce(lambda a, b: a + b, moving)
        counts[term] = jnp.full(counts.shape[1:], total, jnp.int32)
        ahead, behind = 0, total
        for p in range(pairs):
            place = jnp.where(moving[p] == 1, ahead, behind)
            ahead, behind = ahead + moving[p], behind + 1 - moving[p]
            columns = pl.ds(pl.multiple_of(place * size, 128), size)
            left = jnp.where(own, left_own[p], left_other[p])
            right = jnp.where(own, right_own[p], right_other[p])
            rights[term, :, columns] = right.T if term == 0 else right
            lefts[term, :, columns] = left if term == 0 else left.T


def arrange(slot, steps, lefts, rights, *pieces):
    pairs, size, _ = lefts[0].shape
    rows, width = pieces[0].shape
    shape = jax.ShapeDtypeStruct((2, size, pairs * size), lefts[0].dtype)
    counts = jax.ShapeDtypeStruct((2, 8, 128), jnp.int32)
    return pl.pallas_call(
        functools.partial(arrange_kernel, slot),
        out_shape=(shape, shape, counts, jax.ShapeDtypeStruct((rows, width * len(pieces)), pieces[0].dtype)),
        in_specs=[SMEM] * 2 + [VMEM] * (4 + len(pieces)),
        out_specs=(VMEM,) * 4,
        compiler_params=pltpu.CompilerParams(vmem_limit_bytes=LIMIT),
        cost_estimate=pl.CostEstimate(flops=COST, bytes_accessed=1, transcendentals=0),
        name="arrange",
    )(*steps, *lefts, *rights, *pieces)


def chunks(size, parts):
    rows = size // parts
    if rows % 16:
        return [(0, 0, size)]
    bits = parts.bit_length() - 1
    return [(i * rows, mirrored(i, bits) * rows, rows) for i in range(parts)]


def put(ref, value, parts):
    for natural, at, rows in chunks(value.shape[0], parts):
        ref[at : at + rows] = value[natural : natural + rows].astype(ref.dtype)


def one_term(parts, term, counts, vector, lefts, rights, middle, moved, stayed):
    size = vector.shape[0]
    pairs = middle.shape[0] // size
    movers = jnp.where(term == 0, jnp.max(counts[0]), jnp.max(counts[1]))
    step = 2 if pairs % 2 == 0 else 1
    for first in range(0, pairs, step):
        columns = slice(first * size, (first + step) * size)
        turned = jnp.dot(vector[...], rights[term, :, columns], preferred_element_type=jnp.float32)
        turned = turned.astype(middle.dtype)
        for p in range(step):
            for natural, at, rows in chunks(size, parts):
                to = (first + p) * size + natural
                middle[to : to + rows] = turned[at : at + rows, p * size : (p + 1) * size]
    for count in range(pairs + 1):

        @pl.when(movers == count)
        def _(cut=count * size):
            def total(part):
                if part.start == part.stop:
                    return None
                return jnp.dot(lefts[term, :, part], middle[part], preferred_element_type=jnp.float32)

            if moved is not None:
                moved(total(slice(0, cut)))
            stayed(total(slice(cut, pairs * size)))


def none_or(total, base):
    if total is None:
        return base
    return total if base is None else total + base


def inner_kernel(parts, with_cross, counts, vector, lefts, rights, near, stayed, *rest):
    cross, middle = rest if with_cross else (None, *rest)
    size = vector.shape[0]
    zeros = functools.partial(jnp.zeros, (size, size), jnp.float32)
    term = outer_slot()

    def set_near(total):
        near[...] = zeros() if total is None else total

    def set_stayed(total):
        stayed[...] = zeros() if total is None else total

    def set_cross(total):
        put(cross, zeros() if total is None else total, parts)

    def add_stayed(total):
        if total is not None:
            stayed[...] += total

    one_term(parts, 1 - term, counts, vector, lefts, rights, middle, set_near, set_stayed)
    one_term(
        parts, term, counts, vector, lefts, rights, middle, set_cross if with_cross else None, add_stayed
    )


def first_kernel(parts, counts, vector, lefts, rights, cross, stayed, middle):
    size = vector.shape[0]
    zeros = functools.partial(jnp.zeros, (size, size), jnp.float32)

    def set_cross(total):
        put(cross, zeros() if total is None else total, parts)

    def set_stayed(total):
        stayed[...] = zeros() if total is None else total

    one_term(parts, 1 - outer_slot(), counts, vector, lefts, rights, middle, set_cross, set_stayed)


def second_kernel(parts, counts, vector, lefts, rights, stayed, near_in, stayed_in, own, other, middle):
    def set_other(total):
        put(other, none_or(total, stayed_in[...]), parts)

    def set_own(total):
        put(own, none_or(total, stayed[...] + near_in[...]), parts)

    one_term(parts, outer_slot(), counts, vector, lefts, rights, middle, set_other, set_own)


def merge_kernel(own, arrived, other, *rest):
    more, outer, inner = rest if len(rest) == 3 else (None, *rest)
    outer[...] = (own[...] + arrived[...].astype(jnp.float32)).astype(outer.dtype)
    total = other[...]
    if more is not None:
        total = total + more[...].astype(jnp.float32)
    inner[...] = total.astype(inner.dtype)


def merge(own, arrived, other, *more):
    shape = jax.ShapeDtypeStruct(own.shape, jnp.bfloat16)
    return pl.pallas_call(
        merge_kernel,
        out_shape=(shape, shape),
        in_specs=[VMEM] * (3 + len(more)),
        out_specs=(VMEM, VMEM),
        compiler_params=pltpu.CompilerParams(vmem_limit_bytes=LIMIT),
        cost_estimate=pl.CostEstimate(flops=1, bytes_accessed=1, transcendentals=0),
        name="merge",
    )(own, arrived, other, *more)


def call(kernel, name, kinds, cost, vector, weights, *more):
    lefts, rights, counts = weights
    size, width = lefts.shape[1:]
    shapes = tuple(jax.ShapeDtypeStruct((size, size), kind) for kind in kinds)
    return pl.pallas_call(
        kernel,
        out_shape=shapes,
        in_specs=[VMEM] * (4 + len(more)),
        out_specs=(VMEM,) * len(shapes),
        scratch_shapes=[pltpu.VMEM((width, size), jnp.bfloat16)],
        compiler_params=pltpu.CompilerParams(vmem_limit_bytes=LIMIT),
        cost_estimate=pl.CostEstimate(flops=cost, bytes_accessed=1, transcendentals=0),
        name=name,
    )(counts, vector, lefts, rights, *more)


def on_device(wavefunction, diagonal, left_ops, right_ops, offsets):
    members = lax.axis_size("op")
    sectors = lax.axis_size("sec")
    bits = members.bit_length() - 1
    steps = [1 << k for k in range(bits)]
    groups, last = [steps[k : min(k + 2, bits - 1)] for k in range(0, bits - 1, 2)], steps[-1]
    sides = {d: side("op", d) for d in steps}
    shard, width = wavefunction.shape[2:]
    size = members * shard
    core = side("sec", 1)
    bf16, f32 = jnp.bfloat16, jnp.float32
    pair = sectors == 4
    mine = core == outer_slot()

    def both_slots(own, other):
        return jnp.where(mine, own, other), jnp.where(mine, other, own)

    def position(group):
        return functools.reduce(lambda a, d: 2 * a + sides[d], group, 0)

    def partners(group):
        count = 1 << len(group)
        return [(j, sum(d for k, d in enumerate(group) if j >> (len(group) - 1 - k) & 1)) for j in range(count - 1, 0, -1)]

    def scatter(block, group):
        rows = block.shape[0] >> len(group)
        place = position(group)
        sent = [lax.dynamic_slice_in_dim(block, (place ^ j) * rows, rows) for j, _ in partners(group)]
        arrived = [swap(piece, "op", distance) for piece, (_, distance) in zip(sent, partners(group))]
        total = lax.dynamic_slice_in_dim(block, place * rows, rows).astype(f32)
        for piece in arrived:
            total = total + piece.astype(f32)
        return total

    def gather(block, group, own=None):
        rows = block.shape[0]
        place = position(group)
        first_arrived = None
        whole = jnp.zeros((rows << len(group), block.shape[1]), block.dtype)
        whole = lax.dynamic_update_slice_in_dim(whole, block if own is None else own, place * rows, 0)
        for j, distance in partners(group):
            piece = swap(block, "op", distance)
            first_arrived = piece if first_arrived is None else first_arrived
            whole = lax.dynamic_update_slice_in_dim(whole, piece, (place ^ j) * rows, 0)
        return whole, first_arrived

    def respread(block):
        if shard % 16 == 0:
            return block
        spread = block.reshape((2,) * bits + (shard, -1))
        return spread.transpose(tuple(range(bits))[::-1] + (bits, bits + 1)).reshape(block.shape)

    def gather_all(block):
        for group in groups[::-1]:
            block, first_arrived = gather(block, group)
        return respread(block), first_arrived

    def beside(block, own=None):
        own = block if own is None else own
        arrived = swap(block, "op", last)
        low = jnp.where(sides[last] == 0, own, arrived)
        high = jnp.where(sides[last] == 0, arrived, own)
        return jnp.concatenate([low, high])

    own_roots = wavefunction[0]
    other_roots = swap(own_roots, "sec", 1)
    own_root = jnp.where(core == 0, own_roots[0], own_roots[1])
    other_root = jnp.where(core == 0, other_roots[0], other_roots[1])
    start = jnp.concatenate(both_slots(own_root, other_root), axis=1)
    start, left_given, right_given = lax.optimization_barrier((start, left_ops, right_ops))
    lefts = (left_ops, swap(left_given, "sec", 1))
    rights = (right_ops, swap(right_given, "sec", 1))
    moves = (offsets, swap(offsets, "sec", 1))
    *outer_weights, passed = arrange(0, moves, lefts, rights, start)
    together = beside(start, passed)
    together, own_diagonal = lax.optimization_barrier((together, diagonal[0]))
    together, _ = gather_all(together)
    vectors = [together[:, :width], together[:, width:]]
    *inner_weights, slots = arrange(1, moves, lefts, rights, own_diagonal, swap(own_diagonal, "sec", 1))
    both_diagonals = beside(slots)
    own_diagonals = [slots[:, :width], slots[:, width:]]
    diagonals = [both_diagonals[:, :width], both_diagonals[:, width:]]

    for turn in range(ITERS):
        cross, stayed = call(
            functools.partial(first_kernel, members), "first", (bf16, f32), COST, vectors[0], outer_weights
        )
        kinds = (f32, f32) if pair else (f32, f32, bf16)
        inner = call(functools.partial(inner_kernel, members, not pair), "inner", kinds, COST, vectors[1], inner_weights)
        if pair:
            arrived = (swap(respread(cross), "sec", 2),)
        else:
            arrived = (
                lax.ppermute(respread(inner[2]), "sec", [(i, i + 2) for i in range(sectors - 2)]),
                lax.ppermute(respread(cross), "sec", [(i, i - 2) for i in range(2, sectors)]),
            )
        own, other = call(
            functools.partial(second_kernel, members),
            "second",
            (f32, f32),
            COST//10,
            vectors[0],
            outer_weights,
            stayed,
            inner[0],
            inner[1],
        )
        blocks = list(merge(respread(own), arrived[0], respread(other), *arrived[1:]))
        for k in (0, 1):
            block = blocks[k]
            for group in groups:
                block = scatter(block, group).astype(bf16)
            if turn < ITERS - 1:
                total = block.astype(f32) + swap(block, "op", last).astype(f32)
                ready = (total / diagonals[k]).astype(bf16)
                if k == 1:
                    ready, _ = lax.optimization_barrier((ready, first_arrived))
                vectors[k], first_arrived = gather_all(ready)
            else:
                blocks[k] = (scatter(block, [last]) / own_diagonals[k]).astype(bf16)
    kept = jnp.where(mine, blocks[0], blocks[1])
    returned = swap(jnp.where(mine, blocks[1], blocks[0]), "sec", 1)
    out = jnp.where(core == 0, jnp.stack([kept, returned]), jnp.stack([returned, kept]))
    return out[None]


def solution(mesh):
    in_specs = (
        P("sec", None, "op", None),
        P("sec", "op", None),
        P(("sec", "op"), None, None),
        P(("sec", "op"), None, None),
        P(("sec", "op"), None),
    )
    out_specs = P("sec", None, "op", None)
    return jax.shard_map(
        on_device, mesh=mesh, in_specs=in_specs, out_specs=out_specs, check_vma=False
    )
```
